32 devices in a mesh: grp: 2 (over y), tp: 4 (over z), ap: 2 (over x), sq: 2 (over core).
Axes of the slice: x: 2, y: 2, z: 4, core: 2. Of those that a mesh axis runs over, the one named last changes fastest.
Arguments:
- heads_out: bfloat16 [4096, 8192], P(('grp', 'ap', 'sq'), 'tp'), parts along dimension 0, may hold values from -6 to 6
- base_weight: bfloat16 [8192, 8192], P('tp'), may hold values from -0.09375 to 0.09375
- shrink_store: bfloat16 [32, 64, 8192], P('ap', None, 'tp'), may hold values from -0.0625 to 0.0625
- expand_store: bfloat16 [32, 64, 8192], P('ap', None, 'tp'), may hold values from -0.75 to 0.75
- request_adapter: int32 [16], P(('grp', 'ap', 'sq')), parts along dimension 0, may hold values from 0 to 31
- adapter_slot: int32 [32], replicated, may hold values from 0 to 31, each once
- prompt_length: int32 [16], P(('grp', 'ap', 'sq')), parts along dimension 0, may hold values from 1 to 256, as said below
Outputs:
- projected: bfloat16 [4096, 8192], P(('grp', 'ap', 'sq'), 'tp'), parts along dimension 0
The draws below stay inside these ranges and needn't reach their ends.
There are 2 independent parts, one for each index of `grp`. The reference program is written for one: setup_inputs(seed, part) draws one part's arguments, and reference() takes and returns one part's arrays. A program takes and returns all parts, laid end to end along the dimension named above; an argument that names none is the same for every part. Nothing has to cross between parts.
Inputs may be any that keep to these rules, and one draw needn't show every extreme that they name: `prompt_length`: among the 2 requests of each device one has the full length 256. `adapter_slot`: each slot appears once.
All inputs are finite; a program needn't handle non-finite values.
Results may differ from the reference program's by a relative error of at most 0.001.
Values may be sent and summed in bfloat16 or wider, within the bound.
A program may use at most 192 MiB of HBM per device.

```python
import math
import jax
import jax.numpy as jnp
import numpy as np
from jax import lax

D = 8192
R = 64
SEQ = 256
REQ_DEV = 2
ADAPTERS = 32
REQUESTS = 8
TOKENS = 2048


def draw_prompt_length(key, part):
    key = jax.random.fold_in(key, 7)
    first_key, second_key = jax.random.split(key)
    lengths = jax.random.randint(first_key, (REQUESTS,), 1, SEQ + 1)
    chosen = jax.random.randint(second_key, (REQUESTS // REQ_DEV,), 0, REQ_DEV)
    position = jnp.arange(REQUESTS, dtype=jnp.int32) % REQ_DEV
    full_one = position == jnp.repeat(chosen, REQ_DEV, total_repeat_length=REQUESTS)
    return jnp.where(full_one, SEQ, lengths).astype(jnp.int32)


def touch_ends(array, stream_key, smallest, top_value):
    index_at = [jax.random.randint(jax.random.fold_in(stream_key, axis), (), 0, length) for axis, length in enumerate(array.shape)]
    widest = array.shape.index(max(array.shape))
    beside = index_at[:widest] + [(index_at[widest] + 1) % array.shape[widest]] + index_at[widest + 1:]
    return array.at[tuple(index_at)].set(smallest).at[tuple(beside)].set(top_value)


def spiked(result, own_key, source, target, parts, factor):
    def block_of(dim):
        return (jnp.arange(result.shape[dim]) // (result.shape[dim] // parts)).reshape((-1,) + (1,) * (result.ndim - 1 - dim))

    near = jax.random.permutation(own_key, parts)[block_of(target)]
    far = (block_of(target) + parts // 2) % parts
    return jnp.where((block_of(source) == near) | (block_of(source) == far), factor * result, result)


def block_levels(own_key, extent, pieces, smallest, top_value):
    gain = 1.0
    for axis_at, blocks in pieces:
        heights = jax.random.uniform(jax.random.fold_in(jax.random.fold_in(own_key, 6), axis_at), (blocks,), jnp.float32, smallest / len(pieces), top_value / len(pieces))
        gain = gain * jnp.repeat(jnp.exp(heights), extent[axis_at] // blocks).reshape((-1,) + (1,) * (len(extent) - 1 - axis_at))
    return gain


def cumulative_ranks(count, lean):
    portions = [(1 << 20) // math.isqrt(grade ** lean) + 1 for grade in range(1, count + 1)]
    width = 1 + sum(portions) // (1 << 30)
    return np.cumsum(np.array([max(1, weight // width) for weight in portions]))


def skewed_ids(key, shape, amount, slope):
    table = cumulative_ranks(amount, slope)
    lot = jax.random.randint(jax.random.fold_in(key, 1), shape, 0, int(table[amount - 1]))
    grade = jnp.searchsorted(jnp.asarray(table, jnp.int32), lot, side="right")
    return jax.random.permutation(jax.random.fold_in(key, 2), amount)[grade].astype(jnp.int32)


def centred(stream_key, extent, width, reach, pieces=(), kind=jnp.bfloat16):
    values = jax.random.normal(stream_key, extent, jnp.float32) * width
    if len(pieces) > 0:
        values = block_levels(stream_key, extent, pieces, -0.22, 0.18) * values
    return jnp.clip(values, min=-reach, max=reach).astype(kind)


def gaussian_with(own_key, dims, width, most, cuts, heavy, kind=jnp.bfloat16):
    entries = width * jax.random.normal(own_key, dims, jnp.float32)
    if cuts:
        entries = entries * block_levels(own_key, dims, cuts, -0.22, 0.18)
    return jnp.clip(spiked(entries, jax.random.fold_in(own_key, 3), *heavy), -most, most).astype(kind)


def setup_inputs(seed: int = 0, part: int = 0) -> dict:
    splits = jax.random.split(jax.random.key(seed), 8)
    part_splits = jax.random.split(jax.random.fold_in(splits[7], part), 8)
    return {
        "heads_out": centred(part_splits[0], (TOKENS, D), 1.0, 6.0, ((0, 4), (1, 4))),
        "base_weight": gaussian_with(splits[1], (D, D), D ** -0.5, 0.09375, ((0, 4),), (0, 1, 4, 2.0)),
        "shrink_store": centred(splits[2], (ADAPTERS, R, D), D ** -0.5, 0.0625, ((0, 2), (2, 4))),
        "expand_store": centred(splits[3], (ADAPTERS, R, D), R ** -0.5, 0.75, ((0, 2), (2, 4))),
        "request_adapter": touch_ends(skewed_ids(part_splits[4], (REQUESTS,), ADAPTERS, 2), jax.random.fold_in(part_splits[4], 3), 0, ADAPTERS - 1).astype(jnp.int32),
        "adapter_slot": jax.random.permutation(splits[5], ADAPTERS).astype(jnp.int32),
        "prompt_length": draw_prompt_length(jax.random.fold_in(jax.random.fold_in(splits[7], part), 71), part),
    }


def reference(heads_out, base_weight, shrink_store, expand_store, request_adapter, adapter_slot, prompt_length):
    slot_ids = adapter_slot[request_adapter].astype(jnp.int32)
    base_sum = jnp.dot(heads_out, base_weight, preferred_element_type=jnp.float32)
    blocks = heads_out.reshape(REQUESTS, SEQ, D)

    def per_request(item):
        block, slot_one = item
        down_rows = shrink_store[slot_one]
        up_rows = expand_store[slot_one].astype(jnp.float32)
        rank_act = jnp.dot(block, down_rows.T, preferred_element_type=jnp.float32)
        return jnp.dot(rank_act, up_rows, precision=lax.Precision.HIGHEST)

    expanded = lax.map(per_request, (blocks, slot_ids))
    total = base_sum.reshape(REQUESTS, SEQ, D) + expanded
    live = jnp.arange(SEQ, dtype=jnp.int32)[None, :] < prompt_length[:, None]
    total = jnp.where(live[:, :, None], total, jnp.float32(0.0))
    return total.reshape(TOKENS, D).astype(jnp.bfloat16)
```

```python
import functools

import jax
import jax.numpy as jnp
from jax import lax
from jax.experimental import pallas as pl
from jax.experimental.pallas import tpu as pltpu
from jax.sharding import PartitionSpec as P

MESH = pl.DeviceIdType.MESH
SLOTS = 3
TOP = 32500.0
STEPS = 64.0


def decode(ref, rows):
    power = ref[rows : rows + 16, :][0:1, :].astype(jnp.float32)
    scale = jnp.exp2(power * (1.0 / STEPS)) * (1.0 / TOP)
    return ref[0:rows, :].astype(jnp.float32) * scale


def encode(ref, value, rows):
    top = jnp.maximum(jnp.max(jnp.abs(value), axis=0, keepdims=True), 1e-30)
    power = jnp.ceil(jnp.log2(top) * STEPS)
    factor = jnp.exp2(power * (-1.0 / STEPS)) * TOP
    ref[0:rows, :] = jnp.round(value * factor).astype(jnp.int32).astype(jnp.int16)
    ref[rows : rows + 16, :] = (
        jnp.broadcast_to(power, (16, power.shape[1])).astype(jnp.int32).astype(jnp.int16)
    )


def line_kernel(
    n, chunks, cw, x_ref, w_ref, o_ref, inbox, outbox, wbuf, own_w, acc, recv_sem, send_sem, w_sem, own_sem
):
    i = lax.axis_index("tp")
    rows, depth = x_ref.shape
    bw = chunks * cw
    items = chunks * (n - 1)
    count_right = chunks * (n - 1 - i)
    count_left = chunks * i

    def weight_copy(way, k):
        block = jnp.where(way == 0, n - 1 - k // chunks, k // chunks)
        start = pl.multiple_of(block * bw + (k % chunks) * cw, cw)
        return pltpu.make_async_copy(
            w_ref.at[:, pl.ds(start, cw)], wbuf.at[way, k % 2], w_sem.at[way, k % 2]
        )

    def own_copy(c):
        start = pl.multiple_of(i * bw + c * cw, cw)
        return pltpu.make_async_copy(
            w_ref.at[:, pl.ds(start, cw)], own_w.at[c % 2], own_sem.at[c % 2]
        )

    def item_copy(way, k):
        target = jnp.clip(i + 1 - 2 * way, 0, n - 1)
        return pltpu.make_async_remote_copy(
            src_ref=outbox.at[way, k % SLOTS],
            dst_ref=inbox.at[way, k],
            send_sem=send_sem.at[way, k % SLOTS],
            recv_sem=recv_sem.at[way, k],
            device_id={"tp": target},
            device_id_type=MESH,
        )

    def count_of(way):
        return jnp.where(way == 0, count_right, count_left)

    @pl.when(count_right > 0)
    def _():
        weight_copy(0, 0).start()

    @pl.when(count_left > 0)
    def _():
        weight_copy(1, 0).start()

    own_copy(0).start()

    barrier = pltpu.get_barrier_semaphore()

    @pl.when(i > 0)
    def _():
        pl.semaphore_signal(barrier, inc=1, device_id={"tp": i - 1}, device_id_type=MESH)

    @pl.when(i < n - 1)
    def _():
        pl.semaphore_signal(barrier, inc=1, device_id={"tp": i + 1}, device_id_type=MESH)

    pl.semaphore_wait(barrier, jnp.where(i > 0, 1, 0) + jnp.where(i < n - 1, 1, 0))

    late = jnp.where(i >= n // 2, 1, 0)

    def step(t, carry):
        k = t // 2
        way = (t + late) % 2
        count = count_of(way)

        @pl.when(k < count)
        def _():
            weight_copy(way, k).wait()

            @pl.when(k + 1 < count)
            def _():
                weight_copy(way, k + 1).start()

            acc[...] = jnp.dot(
                x_ref[...], wbuf[way, k % 2], preferred_element_type=jnp.float32
            )

            @pl.when(jnp.where(way == 0, i, n - 1 - i) > 0)
            def _():
                item_copy(way, k).wait_recv()
                acc[...] += decode(inbox.at[way, k], rows)

            @pl.when(k >= SLOTS)
            def _():
                item_copy(way, k).wait_send()

            encode(outbox.at[way, k % SLOTS], acc[...], rows)
            item_copy(way, k).start()

        return carry

    lax.fori_loop(0, 2 * items, step, 0)

    def finish(c, carry):
        own_copy(c).wait()

        @pl.when(c + 1 < chunks)
        def _():
            own_copy(c + 1).start()

        acc[...] = jnp.dot(x_ref[...], own_w[c % 2], preferred_element_type=jnp.float32)

        @pl.when(i > 0)
        def _():
            k = count_right + c
            item_copy(0, k).wait_recv()
            acc[...] += decode(inbox.at[0, k], rows)

        @pl.when(i < n - 1)
        def _():
            k = count_left + c
            item_copy(1, k).wait_recv()
            acc[...] += decode(inbox.at[1, k], rows)

        o_ref[:, pl.ds(pl.multiple_of(c * cw, cw), cw)] = acc[...]
        return carry

    lax.fori_loop(0, chunks, finish, 0)

    def drain(t, carry):
        way = t // SLOTS
        count = count_of(way)
        k = count - 1 - t % SLOTS

        @pl.when(k >= 0)
        def _():
            item_copy(way, k).wait_send()

        return carry

    lax.fori_loop(0, 2 * SLOTS, drain, 0)


def line_sum(n, heads_out, base_weight):
    rows, depth = heads_out.shape
    width = base_weight.shape[1]
    bw = width // n
    cw = min(256, bw)
    chunks = bw // cw
    items = chunks * (n - 1)
    return pl.pallas_call(
        functools.partial(line_kernel, n, chunks, cw),
        out_shape=jax.ShapeDtypeStruct((rows, bw), jnp.float32),
        in_specs=[
            pl.BlockSpec(memory_space=pltpu.VMEM),
            pl.BlockSpec(memory_space=pl.ANY),
        ],
        out_specs=pl.BlockSpec(memory_space=pltpu.VMEM),
        scratch_shapes=[
            pltpu.VMEM((2, items, rows + 16, cw), jnp.int16),
            pltpu.VMEM((2, SLOTS, rows + 16, cw), jnp.int16),
            pltpu.VMEM((2, 2, depth, cw), jnp.bfloat16),
            pltpu.VMEM((2, depth, cw), jnp.bfloat16),
            pltpu.VMEM((rows, cw), jnp.float32),
            pltpu.SemaphoreType.DMA((2, items)),
            pltpu.SemaphoreType.DMA((2, SLOTS)),
            pltpu.SemaphoreType.DMA((2, 2)),
            pltpu.SemaphoreType.DMA((2,)),
        ],
        compiler_params=pltpu.CompilerParams(
            collective_id=0, has_side_effects=True, vmem_limit_bytes=48 * 1024 * 1024
        ),
        cost_estimate=pl.CostEstimate(
            flops=2 * rows * depth * width,
            bytes_accessed=2 * depth * width,
            transcendentals=0,
        ),
    )(heads_out, base_weight)


def on_device(
    n, heads_out, base_weight, shrink_store, expand_store, request_adapter, adapter_slot, prompt_length
):
    req_count = request_adapter.shape[0]
    slot_rows = heads_out.shape[0] // req_count
    width_part = heads_out.shape[1]
    held = shrink_store.shape[0]

    slot_ids = adapter_slot[request_adapter]
    wanted = lax.all_gather(slot_ids, "ap") - lax.axis_index("ap") * held
    here = ((wanted >= 0) & (wanted < held))[:, :, None, None]
    place = jnp.clip(wanted, 0, held - 1)
    zero = jnp.zeros((), shrink_store.dtype)
    picked = jnp.stack(
        [jnp.where(here, store[place], zero) for store in (shrink_store, expand_store)], axis=1
    )
    moved = lax.all_to_all(picked, "ap", 0, 0)
    factors = jnp.sum(moved.astype(jnp.float32), axis=0).astype(jnp.bfloat16)
    down, up = factors[0], factors[1]

    blocks = heads_out.reshape(req_count, slot_rows, width_part)
    rank_part = jnp.einsum("qsd,qkd->qsk", blocks, down, preferred_element_type=jnp.float32)
    rank_act = lax.psum(rank_part, "tp")
    base_share = line_sum(n, heads_out, base_weight)
    expanded = jnp.einsum(
        "qsk,qkn->qsn", rank_act, up.astype(jnp.float32), precision=lax.Precision.HIGHEST
    )
    total = base_share.reshape(req_count, slot_rows, -1) + expanded
    live = jnp.arange(slot_rows, dtype=jnp.int32)[None, :] < prompt_length[:, None]
    total = jnp.where(live[:, :, None], total, jnp.float32(0.0))
    return total.reshape(req_count * slot_rows, -1).astype(jnp.bfloat16)


def solution(mesh):
    return jax.shard_map(
        functools.partial(on_device, mesh.shape["tp"]),
        mesh=mesh,
        in_specs=(
            P(("grp", "ap", "sq"), "tp"),
            P("tp", None),
            P("ap", None, "tp"),
            P("ap", None, "tp"),
            P(("grp", "ap", "sq")),
            P(),
            P(("grp", "ap", "sq")),
        ),
        out_specs=P(("grp", "ap", "sq"), "tp"),
        check_vma=False,
    )
```

```python
import functools

import jax
import jax.numpy as jnp
from jax import lax
from jax.experimental import pallas as pl
from jax.experimental.pallas import tpu as pltpu
from jax.sharding import PartitionSpec as P

MESH = pl.DeviceIdType.MESH
SLOTS = 3
TOP = 32500.0
STEPS = 64.0


def decode(ref, rows):
    power = ref[rows : rows + 16, :][0:1, :].astype(jnp.float32)
    scale = jnp.exp2(power * (1.0 / STEPS)) * (1.0 / TOP)
    return ref[0:rows, :].astype(jnp.float32) * scale


def encode(ref, value, rows):
    top = jnp.maximum(jnp.max(jnp.abs(value), axis=0, keepdims=True), 1e-30)
    power = jnp.ceil(jnp.log2(top) * STEPS)
    factor = jnp.exp2(power * (-1.0 / STEPS)) * TOP
    ref[0:rows, :] = jnp.round(value * factor).astype(jnp.int32).astype(jnp.int16)
    ref[rows : rows + 16, :] = (
        jnp.broadcast_to(power, (16, power.shape[1])).astype(jnp.int32).astype(jnp.int16)
    )


def line_kernel(
    n, n_ap, chunks, cw, req, x_ref, w_ref, picked_ref, length_ref, o_ref, inbox, outbox, wbuf, own_w, acc,
    factors, up, rank_own, rank_in, rank_out, parts, recv_sem, send_sem, w_sem, own_sem,
    factor_recv, factor_send, rank_recv, rank_send, local_sem,
):
    i = lax.axis_index("tp")
    me = lax.axis_index("ap")
    rows, depth = x_ref.shape
    slot_rows, lanes = rank_own.shape
    rank = lanes // req
    bw = chunks * cw
    items = chunks * (n - 1)
    middle = items // 3
    count_right = chunks * (n - 1 - i)
    count_left = chunks * i

    def factor_copy(hop):
        return pltpu.make_async_remote_copy(
            src_ref=picked_ref.at[(me + hop) % n_ap],
            dst_ref=factors.at[me],
            send_sem=factor_send.at[hop],
            recv_sem=factor_recv.at[hop],
            device_id={"ap": (me + hop) % n_ap},
            device_id_type=MESH,
        )

    def rank_copy(way):
        return pltpu.make_async_remote_copy(
            src_ref=rank_out.at[way],
            dst_ref=rank_in.at[way],
            send_sem=rank_send.at[way],
            recv_sem=rank_recv.at[way],
            device_id={"tp": jnp.clip(i + 1 - 2 * way, 0, n - 1)},
            device_id_type=MESH,
        )

    own_factors = pltpu.make_async_copy(picked_ref.at[me], factors.at[me], local_sem)

    def weight_copy(way, k):
        block = jnp.where(way == 0, n - 1 - k // chunks, k // chunks)
        start = pl.multiple_of(block * bw + (k % chunks) * cw, cw)
        return pltpu.make_async_copy(
            w_ref.at[:, pl.ds(start, cw)], wbuf.at[way, k % 2], w_sem.at[way, k % 2]
        )

    def own_copy(c):
        start = pl.multiple_of(i * bw + c * cw, cw)
        return pltpu.make_async_copy(
            w_ref.at[:, pl.ds(start, cw)], own_w.at[c % 2], own_sem.at[c % 2]
        )

    def item_copy(way, k):
        target = jnp.clip(i + 1 - 2 * way, 0, n - 1)
        return pltpu.make_async_remote_copy(
            src_ref=outbox.at[way, k % SLOTS],
            dst_ref=inbox.at[way, k],
            send_sem=send_sem.at[way, k % SLOTS],
            recv_sem=recv_sem.at[way, k],
            device_id={"tp": target},
            device_id_type=MESH,
        )

    def count_of(way):
        return jnp.where(way == 0, count_right, count_left)

    @pl.when(count_right > 0)
    def _():
        weight_copy(0, 0).start()

    @pl.when(count_left > 0)
    def _():
        weight_copy(1, 0).start()

    own_copy(0).start()
    own_factors.start()

    barrier = pltpu.get_barrier_semaphore()

    @pl.when(i > 0)
    def _():
        pl.semaphore_signal(barrier, inc=1, device_id={"tp": i - 1}, device_id_type=MESH)

    @pl.when(i < n - 1)
    def _():
        pl.semaphore_signal(barrier, inc=1, device_id={"tp": i + 1}, device_id_type=MESH)

    for hop in range(1, n_ap):
        pl.semaphore_signal(
            barrier, inc=1, device_id={"ap": (me + hop) % n_ap}, device_id_type=MESH
        )

    pl.semaphore_wait(
        barrier, n_ap - 1 + jnp.where(i > 0, 1, 0) + jnp.where(i < n - 1, 1, 0)
    )

    for hop in range(1, n_ap):
        factor_copy(hop).start()

    late = jnp.where(i >= n // 2, 1, 0)

    def step(t, carry):
        k = t // 2
        way = (t + late) % 2
        count = count_of(way)

        @pl.when(t == 2 * middle)
        def _():
            own_factors.wait()
            for hop in range(1, n_ap):
                factor_copy(hop).wait_recv()
            down = factors[0, 0]
            grow = factors[0, 1]
            for source in range(1, n_ap):
                down = down + factors[source, 0]
                grow = grow + factors[source, 1]
            up[...] = grow
            full = lax.dot_general(
                x_ref[...], down, (((1,), (1,)), ((), ())), preferred_element_type=jnp.float32
            )
            lane = lax.broadcasted_iota(jnp.int32, (slot_rows, lanes), 1)
            total = full[0:slot_rows]
            for q in range(1, req):
                total = jnp.where(lane >= q * rank, full[q * slot_rows : (q + 1) * slot_rows], total)
            rank_own[...] = total

        @pl.when((k == middle) & (count > 0))
        def _():
            rank_out[way] = rank_own[...]

            @pl.when(jnp.where(way == 0, i, n - 1 - i) > 0)
            def _():
                rank_copy(way).wait_recv()
                rank_out[way] = rank_own[...] + rank_in[way]

            rank_copy(way).start()

        @pl.when(k < count)
        def _():
            weight_copy(way, k).wait()

            @pl.when(k + 1 < count)
            def _():
                weight_copy(way, k + 1).start()

            acc[...] = jnp.dot(
                x_ref[...], wbuf[way, k % 2], preferred_element_type=jnp.float32
            )

            @pl.when(jnp.where(way == 0, i, n - 1 - i) > 0)
            def _():
                item_copy(way, k).wait_recv()
                acc[...] += decode(inbox.at[way, k], rows)

            @pl.when(k >= SLOTS)
            def _():
                item_copy(way, k).wait_send()

            encode(outbox.at[way, k % SLOTS], acc[...], rows)
            item_copy(way, k).start()

        return carry

    lax.fori_loop(0, 2 * items, step, 0)

    @pl.when(i == n - 1)
    def _():
        rank_copy(0).wait_recv()

    @pl.when(i == 0)
    def _():
        rank_copy(1).wait_recv()

    @pl.when(i > 0)
    def _():
        rank_own[...] += rank_in[0]

    @pl.when(i < n - 1)
    def _():
        rank_own[...] += rank_in[1]

    lane = lax.broadcasted_iota(jnp.int32, (slot_rows, lanes), 1)
    for q in range(req):
        left = jnp.where((lane >= q * rank) & (lane < (q + 1) * rank), rank_own[...], 0.0)
        for term in range(3):
            piece = left.astype(jnp.bfloat16)
            parts[term, q * slot_rows : (q + 1) * slot_rows, :] = piece
            left = left - piece.astype(jnp.float32)

    position = lax.broadcasted_iota(jnp.int32, (slot_rows, cw), 0)

    def finish(c, carry):
        own_copy(c).wait()

        @pl.when(c + 1 < chunks)
        def _():
            own_copy(c + 1).start()

        here = pl.ds(pl.multiple_of(c * cw, cw), cw)
        expanded = jnp.zeros((rows, cw), jnp.float32)
        for term in (2, 1, 0):
            expanded += jnp.dot(parts[term], up[:, here], preferred_element_type=jnp.float32)
        acc[...] = expanded + jnp.dot(
            x_ref[...], own_w[c % 2], preferred_element_type=jnp.float32
        )

        @pl.when(i > 0)
        def _():
            k = count_right + c
            item_copy(0, k).wait_recv()
            acc[...] += decode(inbox.at[0, k], rows)

        @pl.when(i < n - 1)
        def _():
            k = count_left + c
            item_copy(1, k).wait_recv()
            acc[...] += decode(inbox.at[1, k], rows)

        for q in range(req):
            span = slice(q * slot_rows, (q + 1) * slot_rows)
            o_ref[span, here] = jnp.where(
                position < length_ref[q], acc[span, :], 0.0
            ).astype(jnp.bfloat16)
        return carry

    lax.fori_loop(0, chunks, finish, 0)

    def drain(t, carry):
        way = t // SLOTS
        count = count_of(way)
        k = count - 1 - t % SLOTS

        @pl.when(k >= 0)
        def _():
            item_copy(way, k).wait_send()

        return carry

    lax.fori_loop(0, 2 * SLOTS, drain, 0)

    for hop in range(1, n_ap):
        factor_copy(hop).wait_send()
    for way in range(2):

        @pl.when(count_of(way) > 0)
        def _():
            rank_copy(way).wait_send()


def line_sum(n, n_ap, heads_out, base_weight, picked, prompt_length):
    rows, depth = heads_out.shape
    width = base_weight.shape[1]
    req = prompt_length.shape[0]
    lanes = picked.shape[2]
    bw = width // n
    cw = min(256, bw)
    chunks = bw // cw
    items = chunks * (n - 1)
    slot_rows = rows // req
    return pl.pallas_call(
        functools.partial(line_kernel, n, n_ap, chunks, cw, req),
        out_shape=jax.ShapeDtypeStruct((rows, bw), jnp.bfloat16),
        in_specs=[
            pl.BlockSpec(memory_space=pltpu.VMEM),
            pl.BlockSpec(memory_space=pl.ANY),
            pl.BlockSpec(memory_space=pl.ANY),
            pl.BlockSpec(memory_space=pltpu.SMEM),
        ],
        out_specs=pl.BlockSpec(memory_space=pltpu.VMEM),
        scratch_shapes=[
            pltpu.VMEM((2, items, rows + 16, cw), jnp.int16),
            pltpu.VMEM((2, SLOTS, rows + 16, cw), jnp.int16),
            pltpu.VMEM((2, 2, depth, cw), jnp.bfloat16),
            pltpu.VMEM((2, depth, cw), jnp.bfloat16),
            pltpu.VMEM((rows, cw), jnp.float32),
            pltpu.VMEM(picked.shape, jnp.bfloat16),
            pltpu.VMEM((lanes, depth), jnp.bfloat16),
            pltpu.VMEM((slot_rows, lanes), jnp.float32),
            pltpu.VMEM((2, slot_rows, lanes), jnp.float32),
            pltpu.VMEM((2, slot_rows, lanes), jnp.float32),
            pltpu.VMEM((3, rows, lanes), jnp.bfloat16),
            pltpu.SemaphoreType.DMA((2, items)),
            pltpu.SemaphoreType.DMA((2, SLOTS)),
            pltpu.SemaphoreType.DMA((2, 2)),
            pltpu.SemaphoreType.DMA((2,)),
            pltpu.SemaphoreType.DMA((n_ap,)),
            pltpu.SemaphoreType.DMA((n_ap,)),
            pltpu.SemaphoreType.DMA((2,)),
            pltpu.SemaphoreType.DMA((2,)),
            pltpu.SemaphoreType.DMA,
        ],
        compiler_params=pltpu.CompilerParams(
            collective_id=0, has_side_effects=True, vmem_limit_bytes=48 * 1024 * 1024
        ),
        cost_estimate=pl.CostEstimate(
            flops=2 * rows * depth * width,
            bytes_accessed=2 * depth * width,
            transcendentals=0,
        ),
    )(heads_out, base_weight, picked, prompt_length)


def on_device(
    n, n_ap, heads_out, base_weight, shrink_store, expand_store, request_adapter, adapter_slot, prompt_length
):
    held, rank, part = shrink_store.shape
    req = request_adapter.shape[0]
    slot_ids = adapter_slot[request_adapter]
    wanted = lax.all_gather(slot_ids, "ap") - lax.axis_index("ap") * held
    here = ((wanted >= 0) & (wanted < held))[:, :, None, None]
    place = jnp.clip(wanted, 0, held - 1)
    zero = jnp.zeros((), shrink_store.dtype)
    picked = jnp.stack(
        [jnp.where(here, store[place], zero) for store in (shrink_store, expand_store)], axis=1
    )
    picked = picked.reshape(n_ap, 2, req * rank, part)
    return line_sum(n, n_ap, heads_out, base_weight, picked, prompt_length)


def solution(mesh):
    return jax.shard_map(
        functools.partial(on_device, mesh.shape["tp"], mesh.shape["ap"]),
        mesh=mesh,
        in_specs=(
            P(("grp", "ap", "sq"), "tp"),
            P("tp", None),
            P("ap", None, "tp"),
            P("ap", None, "tp"),
            P(("grp", "ap", "sq")),
            P(),
            P(("grp", "ap", "sq")),
        ),
        out_specs=P(("grp", "ap", "sq"), "tp"),
        check_vma=False,
    )
```

```python
import functools

import jax
import jax.numpy as jnp
from jax import lax
from jax.experimental import pallas as pl
from jax.experimental.pallas import tpu as pltpu
from jax.sharding import PartitionSpec as P

MESH = pl.DeviceIdType.MESH
SLOTS = 3
TOP = 32500.0


def encode(ref, scale_ref, value):
    top = jnp.maximum(jnp.max(jnp.abs(value), axis=0, keepdims=True), 1e-30)
    scale_ref[...] = top * (1.0 / TOP)
    ref[...] = jnp.round(value * (TOP / top)).astype(jnp.int32).astype(jnp.int16)


def line_kernel(
    n, n_ap, chunks, cw, req, x_ref, w_ref, shrink_ref, expand_ref, adapter_ref, slot_ref, length_ref,
    o_ref, inbox, outbox, in_scale, out_scale, wbuf, own_w, acc,
    stores, ids_in, ids_out, picked, factors, up, rank_own, rank_in, rank_out, parts, recv_sem, send_sem, w_sem, own_sem,
    scale_recv, scale_send, ids_recv, ids_send, factor_recv, factor_send, rank_recv, rank_send, store_sem,
):
    i = lax.axis_index("tp")
    me = lax.axis_index("ap")
    rows, depth = x_ref.shape
    slot_rows, lanes = rank_own.shape
    rank = lanes // req
    bw = chunks * cw
    items = chunks * (n - 1)
    middle = items // 3
    early = min(2, middle)
    count_right = chunks * (n - 1 - i)
    count_left = chunks * i

    def ids_copy(hop):
        return pltpu.make_async_remote_copy(
            src_ref=ids_out,
            dst_ref=ids_in.at[hop],
            send_sem=ids_send.at[hop],
            recv_sem=ids_recv.at[hop],
            device_id={"ap": (me + hop) % n_ap},
            device_id_type=MESH,
        )

    def factor_copy(hop):
        return pltpu.make_async_remote_copy(
            src_ref=picked.at[hop],
            dst_ref=factors.at[hop],
            send_sem=factor_send.at[hop],
            recv_sem=factor_recv.at[hop],
            device_id={"ap": (me + n_ap - hop) % n_ap},
            device_id_type=MESH,
        )

    store_copies = [
        pltpu.make_async_copy(ref, stores.at[which], store_sem.at[which])
        for which, ref in enumerate((shrink_ref, expand_ref))
    ]

    def rank_copy(way):
        return pltpu.make_async_remote_copy(
            src_ref=rank_out.at[way],
            dst_ref=rank_in.at[way],
            send_sem=rank_send.at[way],
            recv_sem=rank_recv.at[way],
            device_id={"tp": jnp.clip(i + 1 - 2 * way, 0, n - 1)},
            device_id_type=MESH,
        )

    held = stores.shape[1]
    own_slots = [slot_ref[adapter_ref[q]] for q in range(req)]

    def weight_copy(way, k):
        block = jnp.where(way == 0, n - 1 - k // chunks, k // chunks)
        start = pl.multiple_of(block * bw + (k % chunks) * cw, cw)
        return pltpu.make_async_copy(
            w_ref.at[:, pl.ds(start, cw)], wbuf.at[way, k % 2], w_sem.at[way, k % 2]
        )

    def own_copy(c):
        start = pl.multiple_of(i * bw + c * cw, cw)
        return pltpu.make_async_copy(
            w_ref.at[:, pl.ds(start, cw)], own_w.at[c % 2], own_sem.at[c % 2]
        )

    def item_copy(way, k):
        target = jnp.clip(i + 1 - 2 * way, 0, n - 1)
        return pltpu.make_async_remote_copy(
            src_ref=outbox.at[way, k % SLOTS],
            dst_ref=inbox.at[way, k],
            send_sem=send_sem.at[way, k % SLOTS],
            recv_sem=recv_sem.at[way, k],
            device_id={"tp": target},
            device_id_type=MESH,
        )

    def scale_copy(way, k):
        target = jnp.clip(i + 1 - 2 * way, 0, n - 1)
        return pltpu.make_async_remote_copy(
            src_ref=out_scale.at[way, k % SLOTS],
            dst_ref=in_scale.at[way, k],
            send_sem=scale_send.at[way, k % SLOTS],
            recv_sem=scale_recv.at[way, k],
            device_id={"tp": target},
            device_id_type=MESH,
        )

    def count_of(way):
        return jnp.where(way == 0, count_right, count_left)

    @pl.when(count_right > 0)
    def _():
        weight_copy(0, 0).start()

    @pl.when(count_left > 0)
    def _():
        weight_copy(1, 0).start()

    own_copy(0).start()
    for copy in store_copies:
        copy.start()
    line = lax.broadcasted_iota(jnp.int32, ids_out.shape, 0)
    listed = jnp.zeros(ids_out.shape, jnp.int32)
    for q in range(req):
        listed = jnp.where(line == q, own_slots[q], listed)
    ids_out[...] = listed

    barrier = pltpu.get_barrier_semaphore()

    @pl.when(i > 0)
    def _():
        pl.semaphore_signal(barrier, inc=1, device_id={"tp": i - 1}, device_id_type=MESH)

    @pl.when(i < n - 1)
    def _():
        pl.semaphore_signal(barrier, inc=1, device_id={"tp": i + 1}, device_id_type=MESH)

    for hop in range(1, n_ap):
        pl.semaphore_signal(
            barrier, inc=1, device_id={"ap": (me + hop) % n_ap}, device_id_type=MESH
        )

    pl.semaphore_wait(
        barrier, n_ap - 1 + jnp.where(i > 0, 1, 0) + jnp.where(i < n - 1, 1, 0)
    )

    for hop in range(1, n_ap):
        ids_copy(hop).start()

    late = jnp.where(i >= n // 2, 1, 0)

    def step(t, carry):
        k = t // 2
        way = (t + late) % 2
        count = count_of(way)

        @pl.when(t == 2 * early)
        def _():
            for copy in store_copies:
                copy.wait()
            for hop in range(n_ap):
                if hop > 0:
                    ids_copy(hop).wait_recv()
                for q in range(req):
                    slot = own_slots[q] if hop == 0 else jnp.max(ids_in[hop, q : q + 1, :])
                    place = slot - me * held
                    here = (place >= 0) & (place < held)
                    place = jnp.clip(place, 0, held - 1)
                    for which in range(2):
                        value = stores[which, place]
                        value = jnp.where(here, value, jnp.zeros_like(value))
                        span = slice(q * rank, (q + 1) * rank)
                        if hop == 0:
                            factors[0, which, span, :] = value
                        else:
                            picked[hop, which, span, :] = value
                if hop > 0:
                    factor_copy(hop).start()

        @pl.when(t == 2 * middle)
        def _():
            for hop in range(1, n_ap):
                factor_copy(hop).wait_recv()
            down = factors[0, 0]
            grow = factors[0, 1]
            for source in range(1, n_ap):
                down = down + factors[source, 0]
                grow = grow + factors[source, 1]
            up[...] = grow
            full = lax.dot_general(
                x_ref[...], down, (((1,), (1,)), ((), ())), preferred_element_type=jnp.float32
            )
            lane = lax.broadcasted_iota(jnp.int32, (slot_rows, lanes), 1)
            total = full[0:slot_rows]
            for q in range(1, req):
                total = jnp.where(lane >= q * rank, full[q * slot_rows : (q + 1) * slot_rows], total)
            rank_own[...] = total

        @pl.when((k == middle) & (count > 0))
        def _():
            rank_out[way] = rank_own[...]

            @pl.when(jnp.where(way == 0, i, n - 1 - i) > 0)
            def _():
                rank_copy(way).wait_recv()
                rank_out[way] = rank_own[...] + rank_in[way]

            rank_copy(way).start()

        @pl.when(k < count)
        def _():
            weight_copy(way, k).wait()

            @pl.when(k + 1 < count)
            def _():
                weight_copy(way, k + 1).start()

            acc[...] = jnp.dot(
                x_ref[...], wbuf[way, k % 2], preferred_element_type=jnp.float32
            )

            @pl.when(jnp.where(way == 0, i, n - 1 - i) > 0)
            def _():
                item_copy(way, k).wait_recv()
                scale_copy(way, k).wait_recv()
                acc[...] += inbox[way, k].astype(jnp.float32) * in_scale[way, k]

            @pl.when(k >= SLOTS)
            def _():
                item_copy(way, k).wait_send()
                scale_copy(way, k).wait_send()

            encode(outbox.at[way, k % SLOTS], out_scale.at[way, k % SLOTS], acc[...])
            scale_copy(way, k).start()
            item_copy(way, k).start()

        return carry

    lax.fori_loop(0, 2 * items, step, 0)

    @pl.when(i == n - 1)
    def _():
        rank_copy(0).wait_recv()

    @pl.when(i == 0)
    def _():
        rank_copy(1).wait_recv()

    @pl.when(i > 0)
    def _():
        rank_own[...] += rank_in[0]

    @pl.when(i < n - 1)
    def _():
        rank_own[...] += rank_in[1]

    lane = lax.broadcasted_iota(jnp.int32, (slot_rows, lanes), 1)
    for q in range(req):
        left = jnp.where((lane >= q * rank) & (lane < (q + 1) * rank), rank_own[...], 0.0)
        for term in range(3):
            piece = left.astype(jnp.bfloat16)
            parts[term, q * slot_rows : (q + 1) * slot_rows, :] = piece
            left = left - piece.astype(jnp.float32)

    position = lax.broadcasted_iota(jnp.int32, (slot_rows, cw), 0)

    def finish(c, carry):
        own_copy(c).wait()

        @pl.when(c + 1 < chunks)
        def _():
            own_copy(c + 1).start()

        here = pl.ds(pl.multiple_of(c * cw, cw), cw)
        expanded = jnp.zeros((rows, cw), jnp.float32)
        for term in (2, 1, 0):
            expanded += jnp.dot(parts[term], up[:, here], preferred_element_type=jnp.float32)
        acc[...] = expanded + jnp.dot(
            x_ref[...], own_w[c % 2], preferred_element_type=jnp.float32
        )

        @pl.when(i > 0)
        def _():
            k = count_right + c
            item_copy(0, k).wait_recv()
            scale_copy(0, k).wait_recv()
            acc[...] += inbox[0, k].astype(jnp.float32) * in_scale[0, k]

        @pl.when(i < n - 1)
        def _():
            k = count_left + c
            item_copy(1, k).wait_recv()
            scale_copy(1, k).wait_recv()
            acc[...] += inbox[1, k].astype(jnp.float32) * in_scale[1, k]

        for q in range(req):
            span = slice(q * slot_rows, (q + 1) * slot_rows)
            o_ref[span, here] = jnp.where(
                position < length_ref[q], acc[span, :], 0.0
            ).astype(jnp.bfloat16)
        return carry

    lax.fori_loop(0, chunks, finish, 0)

    def drain(t, carry):
        way = t // SLOTS
        count = count_of(way)
        k = count - 1 - t % SLOTS

        @pl.when(k >= 0)
        def _():
            item_copy(way, k).wait_send()
            scale_copy(way, k).wait_send()

        return carry

    lax.fori_loop(0, 2 * SLOTS, drain, 0)

    for hop in range(1, n_ap):
        ids_copy(hop).wait_send()
        factor_copy(hop).wait_send()
    for way in range(2):

        @pl.when(count_of(way) > 0)
        def _():
            rank_copy(way).wait_send()


def line_sum(
    n, n_ap, heads_out, base_weight, shrink_store, expand_store, request_adapter, adapter_slot, prompt_length
):
    rows, depth = heads_out.shape
    width = base_weight.shape[1]
    req = prompt_length.shape[0]
    held, rank, part = shrink_store.shape
    lanes = req * rank
    ids_rows = -(-req // 8) * 8
    bw = width // n
    cw = min(256, bw)
    chunks = bw // cw
    items = chunks * (n - 1)
    slot_rows = rows // req
    return pl.pallas_call(
        functools.partial(line_kernel, n, n_ap, chunks, cw, req),
        out_shape=jax.ShapeDtypeStruct((rows, bw), jnp.bfloat16),
        in_specs=[
            pl.BlockSpec(memory_space=pltpu.VMEM),
            pl.BlockSpec(memory_space=pl.ANY),
            pl.BlockSpec(memory_space=pl.ANY),
            pl.BlockSpec(memory_space=pl.ANY),
            pl.BlockSpec(memory_space=pltpu.SMEM),
            pl.BlockSpec(memory_space=pltpu.SMEM),
            pl.BlockSpec(memory_space=pltpu.SMEM),
        ],
        out_specs=pl.BlockSpec(memory_space=pltpu.VMEM),
        scratch_shapes=[
            pltpu.VMEM((2, items, rows, cw), jnp.int16),
            pltpu.VMEM((2, SLOTS, rows, cw), jnp.int16),
            pltpu.VMEM((2, items, 1, cw), jnp.float32),
            pltpu.VMEM((2, SLOTS, 1, cw), jnp.float32),
            pltpu.VMEM((2, 2, depth, cw), jnp.bfloat16),
            pltpu.VMEM((2, depth, cw), jnp.bfloat16),
            pltpu.VMEM((rows, cw), jnp.float32),
            pltpu.VMEM((2, held, rank, part), jnp.bfloat16),
            pltpu.VMEM((n_ap, ids_rows, 128), jnp.int32),
            pltpu.VMEM((ids_rows, 128), jnp.int32),
            pltpu.VMEM((n_ap, 2, lanes, part), jnp.bfloat16),
            pltpu.VMEM((n_ap, 2, lanes, part), jnp.bfloat16),
            pltpu.VMEM((lanes, depth), jnp.bfloat16),
            pltpu.VMEM((slot_rows, lanes), jnp.float32),
            pltpu.VMEM((2, slot_rows, lanes), jnp.float32),
            pltpu.VMEM((2, slot_rows, lanes), jnp.float32),
            pltpu.VMEM((3, rows, lanes), jnp.bfloat16),
            pltpu.SemaphoreType.DMA((2, items)),
            pltpu.SemaphoreType.DMA((2, SLOTS)),
            pltpu.SemaphoreType.DMA((2, 2)),
            pltpu.SemaphoreType.DMA((2,)),
            pltpu.SemaphoreType.DMA((2, items)),
            pltpu.SemaphoreType.DMA((2, SLOTS)),
            pltpu.SemaphoreType.DMA((n_ap,)),
            pltpu.SemaphoreType.DMA((n_ap,)),
            pltpu.SemaphoreType.DMA((n_ap,)),
            pltpu.SemaphoreType.DMA((n_ap,)),
            pltpu.SemaphoreType.DMA((2,)),
            pltpu.SemaphoreType.DMA((2,)),
            pltpu.SemaphoreType.DMA((2,)),
        ],
        compiler_params=pltpu.CompilerParams(
            collective_id=0, has_side_effects=True, vmem_limit_bytes=48 * 1024 * 1024
        ),
        cost_estimate=pl.CostEstimate(
            flops=2 * rows * depth * width,
            bytes_accessed=2 * depth * width,
            transcendentals=0,
        ),
    )(heads_out, base_weight, shrink_store, expand_store, request_adapter, adapter_slot, prompt_length)


def solution(mesh):
    return jax.shard_map(
        functools.partial(line_sum, mesh.shape["tp"], mesh.shape["ap"]),
        mesh=mesh,
        in_specs=(
            P(("grp", "ap", "sq"), "tp"),
            P("tp", None),
            P("ap", None, "tp"),
            P("ap", None, "tp"),
            P(("grp", "ap", "sq")),
            P(),
            P(("grp", "ap", "sq")),
        ),
        out_specs=P(("grp", "ap", "sq"), "tp"),
        check_vma=False,
    )
```

```python
import functools

import jax
import jax.numpy as jnp
from jax import lax
from jax.experimental import pallas as pl
from jax.experimental.pallas import tpu as pltpu
from jax.sharding import PartitionSpec as P

MESH = pl.DeviceIdType.MESH
SLOTS = 3
TOP = 32500.0


def encode(ref, scale_ref, value):
    top = jnp.maximum(jnp.max(jnp.abs(value), axis=0, keepdims=True), 1e-30)
    scale_ref[...] = top * (1.0 / TOP)
    ref[...] = jnp.round(value * (TOP / top)).astype(jnp.int32).astype(jnp.int16)


def line_kernel(
    n, n_ap, chunks, cw, req, x_hbm, w_ref, shrink_ref, expand_ref, adapter_ref, slot_ref, length_ref,
    o_hbm, x_ref, o_ref, inbox, outbox, in_scale, out_scale, wbuf, own_w, acc,
    stores, ids_in, ids_out, picked, factors, up, rank_own, rank_in, rank_out, parts, recv_sem, send_sem, w_sem, own_sem,
    scale_recv, scale_send, ids_recv, ids_send, factor_recv, factor_send, rank_recv, rank_send, store_sem,
    x_sem, o_sem,
):
    i = lax.axis_index("tp")
    me = lax.axis_index("ap")
    rows, depth = x_ref.shape
    slot_rows, lanes = rank_own.shape
    rank = lanes // req
    bw = chunks * cw
    items = chunks * (n - 1)
    middle = max(1, items // 3)
    early = max(1, min(2, middle))
    count_right = chunks * (n - 1 - i)
    count_left = chunks * i

    def ids_copy(hop):
        return pltpu.make_async_remote_copy(
            src_ref=ids_out,
            dst_ref=ids_in.at[hop],
            send_sem=ids_send.at[hop],
            recv_sem=ids_recv.at[hop],
            device_id={"ap": (me + hop) % n_ap},
            device_id_type=MESH,
        )

    def factor_copy(hop):
        return pltpu.make_async_remote_copy(
            src_ref=picked.at[hop],
            dst_ref=factors.at[hop],
            send_sem=factor_send.at[hop],
            recv_sem=factor_recv.at[hop],
            device_id={"ap": (me + n_ap - hop) % n_ap},
            device_id_type=MESH,
        )

    store_copies = [
        pltpu.make_async_copy(ref, stores.at[which], store_sem.at[which])
        for which, ref in enumerate((shrink_ref, expand_ref))
    ]

    def rank_copy(way):
        return pltpu.make_async_remote_copy(
            src_ref=rank_out.at[way],
            dst_ref=rank_in.at[way],
            send_sem=rank_send.at[way],
            recv_sem=rank_recv.at[way],
            device_id={"tp": jnp.clip(i + 1 - 2 * way, 0, n - 1)},
            device_id_type=MESH,
        )

    held = stores.shape[1]
    own_slots = [slot_ref[adapter_ref[q]] for q in range(req)]

    def weight_copy(way, k):
        block = jnp.where(way == 0, n - 1 - k // chunks, k // chunks)
        start = pl.multiple_of(block * bw + (k % chunks) * cw, cw)
        return pltpu.make_async_copy(
            w_ref.at[:, pl.ds(start, cw)], wbuf.at[way, k % 2], w_sem.at[way, k % 2]
        )

    def own_copy(c):
        start = pl.multiple_of(i * bw + c * cw, cw)
        return pltpu.make_async_copy(
            w_ref.at[:, pl.ds(start, cw)], own_w.at[c % 2], own_sem.at[c % 2]
        )

    def item_copy(way, k):
        target = jnp.clip(i + 1 - 2 * way, 0, n - 1)
        return pltpu.make_async_remote_copy(
            src_ref=outbox.at[way, k % SLOTS],
            dst_ref=inbox.at[way, k],
            send_sem=send_sem.at[way, k % SLOTS],
            recv_sem=recv_sem.at[way, k],
            device_id={"tp": target},
            device_id_type=MESH,
        )

    def scale_copy(way, k):
        target = jnp.clip(i + 1 - 2 * way, 0, n - 1)
        return pltpu.make_async_remote_copy(
            src_ref=out_scale.at[way, k % SLOTS],
            dst_ref=in_scale.at[way, k],
            send_sem=scale_send.at[way, k % SLOTS],
            recv_sem=scale_recv.at[way, k],
            device_id={"tp": target},
            device_id_type=MESH,
        )

    def count_of(way):
        return jnp.where(way == 0, count_right, count_left)

    x_copy = pltpu.make_async_copy(x_hbm, x_ref, x_sem)
    x_copy.start()

    @pl.when(count_right > 0)
    def _():
        weight_copy(0, 0).start()

    @pl.when(count_left > 0)
    def _():
        weight_copy(1, 0).start()

    line = lax.broadcasted_iota(jnp.int32, ids_out.shape, 0)
    listed = jnp.zeros(ids_out.shape, jnp.int32)
    for q in range(req):
        listed = jnp.where(line == q, own_slots[q], listed)
    ids_out[...] = listed

    barrier = pltpu.get_barrier_semaphore()

    @pl.when(i > 0)
    def _():
        pl.semaphore_signal(barrier, inc=1, device_id={"tp": i - 1}, device_id_type=MESH)

    @pl.when(i < n - 1)
    def _():
        pl.semaphore_signal(barrier, inc=1, device_id={"tp": i + 1}, device_id_type=MESH)

    for hop in range(1, n_ap):
        pl.semaphore_signal(
            barrier, inc=1, device_id={"ap": (me + hop) % n_ap}, device_id_type=MESH
        )

    pl.semaphore_wait(
        barrier, n_ap - 1 + jnp.where(i > 0, 1, 0) + jnp.where(i < n - 1, 1, 0)
    )

    for hop in range(1, n_ap):
        ids_copy(hop).start()

    x_copy.wait()

    late = jnp.where(i >= n // 2, 1, 0)

    def step(t, carry):
        k = t // 2
        way = (t + late) % 2
        count = count_of(way)

        @pl.when(t == 1)
        def _():
            own_copy(0).start()
            for copy in store_copies:
                copy.start()

        @pl.when(t == 2 * early)
        def _():
            for copy in store_copies:
                copy.wait()
            for hop in range(n_ap):
                if hop > 0:
                    ids_copy(hop).wait_recv()
                for q in range(req):
                    slot = own_slots[q] if hop == 0 else jnp.max(ids_in[hop, q : q + 1, :])
                    place = slot - me * held
                    here = (place >= 0) & (place < held)
                    place = jnp.clip(place, 0, held - 1)
                    for which in range(2):
                        value = stores[which, place]
                        value = jnp.where(here, value, jnp.zeros_like(value))
                        span = slice(q * rank, (q + 1) * rank)
                        if hop == 0:
                            factors[0, which, span, :] = value
                        else:
                            picked[hop, which, span, :] = value
                if hop > 0:
                    factor_copy(hop).start()

        @pl.when(t == 2 * middle)
        def _():
            for hop in range(1, n_ap):
                factor_copy(hop).wait_recv()
            down = factors[0, 0]
            grow = factors[0, 1]
            for source in range(1, n_ap):
                down = down + factors[source, 0]
                grow = grow + factors[source, 1]
            up[...] = grow
            full = lax.dot_general(
                x_ref[...], down, (((1,), (1,)), ((), ())), preferred_element_type=jnp.float32
            )
            lane = lax.broadcasted_iota(jnp.int32, (slot_rows, lanes), 1)
            total = full[0:slot_rows]
            for q in range(1, req):
                total = jnp.where(lane >= q * rank, full[q * slot_rows : (q + 1) * slot_rows], total)
            rank_own[...] = total

        @pl.when((k == middle) & (count > 0))
        def _():
            rank_out[way] = rank_own[...]

            @pl.when(jnp.where(way == 0, i, n - 1 - i) > 0)
            def _():
                rank_copy(way).wait_recv()
                rank_out[way] = rank_own[...] + rank_in[way]

            rank_copy(way).start()

        @pl.when(k < count)
        def _():
            weight_copy(way, k).wait()

            @pl.when(k + 1 < count)
            def _():
                weight_copy(way, k + 1).start()

            acc[...] = jnp.dot(
                x_ref[...], wbuf[way, k % 2], preferred_element_type=jnp.float32
            )

            @pl.when(jnp.where(way == 0, i, n - 1 - i) > 0)
            def _():
                item_copy(way, k).wait_recv()
                scale_copy(way, k).wait_recv()
                acc[...] += inbox[way, k].astype(jnp.float32) * in_scale[way, k]

            @pl.when(k >= SLOTS)
            def _():
                item_copy(way, k).wait_send()
                scale_copy(way, k).wait_send()

            encode(outbox.at[way, k % SLOTS], out_scale.at[way, k % SLOTS], acc[...])
            scale_copy(way, k).start()
            item_copy(way, k).start()

        return carry

    lax.fori_loop(0, 2 * items, step, 0)

    @pl.when(i == n - 1)
    def _():
        rank_copy(0).wait_recv()

    @pl.when(i == 0)
    def _():
        rank_copy(1).wait_recv()

    @pl.when(i > 0)
    def _():
        rank_own[...] += rank_in[0]

    @pl.when(i < n - 1)
    def _():
        rank_own[...] += rank_in[1]

    lane = lax.broadcasted_iota(jnp.int32, (slot_rows, lanes), 1)
    for q in range(req):
        left = jnp.where((lane >= q * rank) & (lane < (q + 1) * rank), rank_own[...], 0.0)
        for term in range(3):
            piece = left.astype(jnp.bfloat16)
            parts[term, q * slot_rows : (q + 1) * slot_rows, :] = piece
            left = left - piece.astype(jnp.float32)

    position = lax.broadcasted_iota(jnp.int32, (slot_rows, cw), 0)

    def out_copy(c):
        here = pl.ds(pl.multiple_of(c * cw, cw), cw)
        return pltpu.make_async_copy(o_ref.at[:, here], o_hbm.at[:, here], o_sem.at[c])

    def finish(c, carry):
        own_copy(c).wait()

        @pl.when(c + 1 < chunks)
        def _():
            own_copy(c + 1).start()

        here = pl.ds(pl.multiple_of(c * cw, cw), cw)
        expanded = jnp.zeros((rows, cw), jnp.float32)
        for term in (2, 1, 0):
            expanded += jnp.dot(parts[term], up[:, here], preferred_element_type=jnp.float32)
        acc[...] = expanded + jnp.dot(
            x_ref[...], own_w[c % 2], preferred_element_type=jnp.float32
        )

        @pl.when(i > 0)
        def _():
            k = count_right + c
            item_copy(0, k).wait_recv()
            scale_copy(0, k).wait_recv()
            acc[...] += inbox[0, k].astype(jnp.float32) * in_scale[0, k]

        @pl.when(i < n - 1)
        def _():
            k = count_left + c
            item_copy(1, k).wait_recv()
            scale_copy(1, k).wait_recv()
            acc[...] += inbox[1, k].astype(jnp.float32) * in_scale[1, k]

        for q in range(req):
            span = slice(q * slot_rows, (q + 1) * slot_rows)
            o_ref[span, here] = jnp.where(
                position < length_ref[q], acc[span, :], 0.0
            ).astype(jnp.bfloat16)
        out_copy(c).start()
        return carry

    lax.fori_loop(0, chunks, finish, 0)

    def drain(t, carry):
        way = t // SLOTS
        count = count_of(way)
        k = count - 1 - t % SLOTS

        @pl.when(k >= 0)
        def _():
            item_copy(way, k).wait_send()
            scale_copy(way, k).wait_send()

        return carry

    lax.fori_loop(0, 2 * SLOTS, drain, 0)

    def leave(c, carry):
        out_copy(c).wait()
        return carry

    lax.fori_loop(0, chunks, leave, 0)

    for hop in range(1, n_ap):
        ids_copy(hop).wait_send()
        factor_copy(hop).wait_send()
    for way in range(2):

        @pl.when(count_of(way) > 0)
        def _():
            rank_copy(way).wait_send()


def line_sum(
    n, n_ap, heads_out, base_weight, shrink_store, expand_store, request_adapter, adapter_slot, prompt_length
):
    rows, depth = heads_out.shape
    width = base_weight.shape[1]
    req = prompt_length.shape[0]
    held, rank, part = shrink_store.shape
    lanes = req * rank
    ids_rows = -(-req // 8) * 8
    bw = width // n
    cw = min(256, bw)
    chunks = bw // cw
    items = chunks * (n - 1)
    slot_rows = rows // req
    return pl.pallas_call(
        functools.partial(line_kernel, n, n_ap, chunks, cw, req),
        out_shape=jax.ShapeDtypeStruct((rows, bw), jnp.bfloat16),
        in_specs=[
            pl.BlockSpec(memory_space=pl.ANY),
            pl.BlockSpec(memory_space=pl.ANY),
            pl.BlockSpec(memory_space=pl.ANY),
            pl.BlockSpec(memory_space=pl.ANY),
            pl.BlockSpec(memory_space=pltpu.SMEM),
            pl.BlockSpec(memory_space=pltpu.SMEM),
            pl.BlockSpec(memory_space=pltpu.SMEM),
        ],
        out_specs=pl.BlockSpec(memory_space=pl.ANY),
        scratch_shapes=[
            pltpu.VMEM((rows, depth), jnp.bfloat16),
            pltpu.VMEM((rows, bw), jnp.bfloat16),
            pltpu.VMEM((2, items, rows, cw), jnp.int16),
            pltpu.VMEM((2, SLOTS, rows, cw), jnp.int16),
            pltpu.VMEM((2, items, 1, cw), jnp.float32),
            pltpu.VMEM((2, SLOTS, 1, cw), jnp.float32),
            pltpu.VMEM((2, 2, depth, cw), jnp.bfloat16),
            pltpu.VMEM((2, depth, cw), jnp.bfloat16),
            pltpu.VMEM((rows, cw), jnp.float32),
            pltpu.VMEM((2, held, rank, part), jnp.bfloat16),
            pltpu.VMEM((n_ap, ids_rows, 128), jnp.int32),
            pltpu.VMEM((ids_rows, 128), jnp.int32),
            pltpu.VMEM((n_ap, 2, lanes, part), jnp.bfloat16),
            pltpu.VMEM((n_ap, 2, lanes, part), jnp.bfloat16),
            pltpu.VMEM((lanes, depth), jnp.bfloat16),
            pltpu.VMEM((slot_rows, lanes), jnp.float32),
            pltpu.VMEM((2, slot_rows, lanes), jnp.float32),
            pltpu.VMEM((2, slot_rows, lanes), jnp.float32),
            pltpu.VMEM((3, rows, lanes), jnp.bfloat16),
            pltpu.SemaphoreType.DMA((2, items)),
            pltpu.SemaphoreType.DMA((2, SLOTS)),
            pltpu.SemaphoreType.DMA((2, 2)),
            pltpu.SemaphoreType.DMA((2,)),
            pltpu.SemaphoreType.DMA((2, items)),
            pltpu.SemaphoreType.DMA((2, SLOTS)),
            pltpu.SemaphoreType.DMA((n_ap,)),
            pltpu.SemaphoreType.DMA((n_ap,)),
            pltpu.SemaphoreType.DMA((n_ap,)),
            pltpu.SemaphoreType.DMA((n_ap,)),
            pltpu.SemaphoreType.DMA((2,)),
            pltpu.SemaphoreType.DMA((2,)),
            pltpu.SemaphoreType.DMA((2,)),
            pltpu.SemaphoreType.DMA,
            pltpu.SemaphoreType.DMA((chunks,)),
        ],
        compiler_params=pltpu.CompilerParams(
            collective_id=0, has_side_effects=True, vmem_limit_bytes=62 * 1024 * 1024
        ),
        cost_estimate=pl.CostEstimate(
            flops=2 * rows * depth * width,
            bytes_accessed=2 * depth * width,
            transcendentals=0,
        ),
    )(heads_out, base_weight, shrink_store, expand_store, request_adapter, adapter_slot, prompt_length)


def solution(mesh):
    return jax.shard_map(
        functools.partial(line_sum, mesh.shape["tp"], mesh.shape["ap"]),
        mesh=mesh,
        in_specs=(
            P(("grp", "ap", "sq"), "tp"),
            P("tp", None),
            P("ap", None, "tp"),
            P("ap", None, "tp"),
            P(("grp", "ap", "sq")),
            P(),
            P(("grp", "ap", "sq")),
        ),
        out_specs=P(("grp", "ap", "sq"), "tp"),
        check_vma=False,
    )
```
